32 devices in a mesh: ka: 8 (over z, y), band: 2 (over x), ga: 2 (over core).
Axes of the slice: x: 2, y: 2, z: 4, core: 2. Of those that a mesh axis runs over, the one named last changes fastest.
Arguments:
- pair_density: bfloat16 [8, 256, 8, 2048], P(None, ('ka', 'band')), may hold values from -4 to 4
- valence_energy: float32 [8, 8], replicated, may hold values from -6 to -1
- conduction_energy: float32 [8, 256], replicated, may hold values from 0.5 to 12
- star_map: int32 [64], replicated, may hold values from 0 to 7, as said below
- op_of_k: int32 [64], replicated, may hold values from 0 to 47
- perm_lists: int32 [48, 2048], replicated, may hold values from 0 to 2047, as said below
- cond_top: int32 [64], replicated, may hold values from 128 to 256
Outputs:
- chi: float32 [1, 2048, 2048], P(None, ('band', 'ga'), 'ka')
The draws below stay inside these ranges and needn't reach their ends.
Inputs may be any that keep to these rules, and one draw needn't show every extreme that they name: `star_map`: every irreducible point is named by at least one full-zone k-point. `perm_lists`: each row is a permutation of 0 .. 2047 that maps every aligned block of 128 slots onto itself.
All inputs are finite; a program needn't handle non-finite values.
Results may differ from the reference program's by a relative error of at most 0.0015.
Values may be sent and summed in bfloat16 or wider, within the bound.
A program may use at most 320 MiB of HBM per device.

```python
import jax
import jax.numpy as jnp
from jax import lax

NV = 8
NC = 256
NG = 2048
GB = 128
KI = 8
KF = 64
NOPS = 48
NF = 1


def draw_star_map(key, part):
    first_key, second_key = jax.random.split(jax.random.fold_in(key, 17))
    extra = jax.random.randint(first_key, (KF - KI,), 0, KI)
    base = jnp.concatenate([jnp.arange(KI), extra]).astype(jnp.int32)
    return jax.random.permutation(second_key, base).astype(jnp.int32)


def draw_cond_top(key, part):
    first_key, second_key = jax.random.split(jax.random.fold_in(key, 29))
    values = jax.random.randint(first_key, (KF,), NC // 2, NC + 1).astype(jnp.int32)
    places = jax.random.permutation(second_key, KF)
    values = values.at[places[0]].set(NC)
    values = values.at[places[1]].set(NC // 2)
    return values.astype(jnp.int32)


def draw_perm_lists(key, part):
    blocks = NG // GB
    keys = jax.random.split(jax.random.fold_in(key, 41), NOPS * blocks)
    shuffled = jax.vmap(lambda item: jax.random.permutation(item, GB))(keys)
    shuffled = shuffled.reshape(NOPS, blocks, GB) + (jnp.arange(blocks) * GB)[None, :, None]
    return shuffled.reshape(NOPS, NG).astype(jnp.int32)


def with_ends(entries, key, smallest, largest):
    index_at = [jax.random.randint(jax.random.fold_in(key, axis), (), 0, length) for axis, length in enumerate(entries.shape)]
    main_axis = entries.shape.index(max(entries.shape))
    next_to = index_at[:main_axis] + [(index_at[main_axis] + 1) % entries.shape[main_axis]] + index_at[main_axis + 1:]
    return entries.at[tuple(index_at)].set(smallest).at[tuple(next_to)].set(largest)


def block_scale(own_key, shape, cuts, smallest, top_value):
    def one(dim, shards_of):
        draws = jax.random.uniform(jax.random.fold_in(jax.random.fold_in(own_key, 6), dim), (shards_of,), jnp.float32, smallest / len(cuts), top_value / len(cuts))
        return jnp.repeat(jnp.exp(draws), shape[dim] // shards_of).reshape((-1,) + (1,) * (len(shape) - dim - 1))

    level = one(*cuts[0])
    for cut in cuts[1:]:
        level = level * one(*cut)
    return level


def scatter_about(rng, extent, spread, reach, shards=(), dtype=jnp.bfloat16):
    array = spread * jax.random.normal(rng, extent, jnp.float32)
    if shards:
        array = array * block_scale(rng, extent, shards, -0.22, 0.18)
    return jnp.clip(array, -reach, reach).astype(dtype)


def setup_inputs(seed: int = 0) -> dict:
    seeds = jax.random.split(jax.random.key(seed), 8)
    pair_density = scatter_about(seeds[0], (KI, NC, NV, NG), 0.5, 4.0, ((1, 16),))
    valence_energy = jnp.clip(jax.random.uniform(seeds[1], (KI, NV), jnp.float32, -6.0, -1.0), -6.0, -1.0)
    conduction_energy = jnp.clip(jax.random.uniform(seeds[2], (KI, NC), jnp.float32, 0.5, 12.0), 0.5, 12.0)
    star_map = draw_star_map(jax.random.fold_in(seeds[7], 71), 0)
    op_of_k = with_ends(jax.random.randint(seeds[4], (KF,), 0, NOPS), jax.random.fold_in(seeds[4], 1), 0, NOPS - 1).astype(jnp.int32)
    perm_lists = draw_perm_lists(jax.random.fold_in(seeds[7], 71), 0)
    cond_top = draw_cond_top(jax.random.fold_in(seeds[7], 71), 0)
    return dict(pair_density=pair_density, valence_energy=valence_energy, conduction_energy=conduction_energy, star_map=star_map, op_of_k=op_of_k, perm_lists=perm_lists, cond_top=cond_top)


freq_step = 2.0


def reference(pair_density, valence_energy, conduction_energy, star_map, op_of_k, perm_lists, cond_top):
    omega = freq_step * jnp.arange(NF).astype(jnp.float32)
    omega_sq = (omega * omega)[:, None, None]
    band_ids = jnp.arange(NC).astype(jnp.int32)

    def accumulate(chi_sum, kpoint):
        source = star_map[kpoint]
        block = pair_density[source]
        rotated = jnp.take(block, perm_lists[op_of_k[kpoint]], axis=2)
        diff = valence_energy[source][None, :] - conduction_energy[source][:, None]
        mask = (band_ids < cond_top[kpoint]).astype(jnp.float32)[None, :, None]
        weight = (4.0 / KF) * diff[None] / (diff[None] * diff[None] + omega_sq) * mask
        product = weight[..., None] * rotated.astype(jnp.float32)[None]
        scaled_hi = product.astype(jnp.bfloat16)
        hi_back = lax.optimization_barrier(scaled_hi).astype(jnp.float32)
        scaled_lo = (product - hi_back).astype(jnp.bfloat16)
        flat = rotated.reshape(NC * NV, NG).astype(jnp.float32)
        flat_hi = scaled_hi.reshape(NF, NC * NV, NG).astype(jnp.float32)
        flat_lo = scaled_lo.reshape(NF, NC * NV, NG).astype(jnp.float32)
        term = jnp.einsum("rg,frh->fgh", flat, flat_hi, precision=lax.Precision.HIGHEST)
        term = term + jnp.einsum("rg,frh->fgh", flat, flat_lo, precision=lax.Precision.HIGHEST)
        return chi_sum + term, None

    start = jnp.zeros((NF, NG, NG), jnp.float32)
    chi, unused = lax.scan(accumulate, start, jnp.arange(KF).astype(jnp.int32))
    return chi
```

```python
import functools
import itertools

import jax
import jax.numpy as jnp
from jax import lax
from jax.experimental import pallas as pl
from jax.experimental.pallas import tpu as pltpu
from jax.sharding import PartitionSpec as P

NV = 8
NG = 2048
GB = 128
KI = 8
KF = 64
BLOCKS = NG // GB
NT = (((1,), (1,)), ((), ()))


def partial_kernel(rows, ct, chunk, bands, gas, star_ref, pd_ref, inv_ref, w_ref, out_ref, rot_ref):
    tile = pl.program_id(0)
    group = max(1, GB // rows)
    wide = group * rows

    @pl.when(tile == 0)
    def rotate():
        targets = lax.broadcasted_iota(jnp.int32, (GB, GB), 0)

        def one_eight(e, carry):
            for sub, b in itertools.product(range(8 // group), range(BLOCKS)):
                start = pl.multiple_of(e * (8 * rows) + sub * wide, wide)
                cols = slice(b * GB, (b + 1) * GB)
                moved = None
                source = inv_ref[pl.ds(pl.multiple_of(e * 8, 8), 8), cols]
                pieces = [pd_ref[star_ref[e * 8 + sub * group + m], :, cols] for m in range(group)]
                for m in range(group):
                    at = sub * group + m
                    if group == 1:
                        x = pieces[0]
                    else:
                        x = jnp.concatenate(
                            [p if n == m else jnp.zeros_like(p) for n, p in enumerate(pieces)], axis=0
                        )
                    onehot = jnp.where(
                        source[at : at + 1] == targets, 1.0, 0.0
                    ).astype(jnp.bfloat16)
                    part = lax.dot_general(onehot, x, NT, preferred_element_type=jnp.float32)
                    moved = part if moved is None else moved + part
                rot_ref[cols, pl.ds(start, wide)] = moved.astype(jnp.bfloat16)
            return carry

        lax.fori_loop(0, KF // 8, one_eight, 0)

    slab = NG // (bands * gas)
    ga = lax.axis_index("ga")
    base = pl.multiple_of(tile * ct, ct)
    out_ref[...] = jnp.zeros_like(out_ref)

    def one_chunk(q, carry):
        ks = pl.ds(pl.multiple_of(q * chunk, chunk), chunk)
        scaled = (rot_ref[pl.ds(base, ct), ks].astype(jnp.float32) * w_ref[:, ks]).astype(jnp.bfloat16)
        for band in range(bands):
            left = rot_ref[pl.ds(pl.multiple_of((band * gas + ga) * slab, slab), slab), ks]
            out_ref[band * slab : (band + 1) * slab, :] += lax.dot_general(
                left, scaled, NT, preferred_element_type=jnp.float32
            )
        return carry

    lax.fori_loop(0, (KF * rows) // chunk, one_chunk, 0)


def on_device(
    pair_density, valence_energy, conduction_energy, star_map, op_of_k, perm_lists, cond_top
):
    bands = lax.axis_size("band")
    gas = lax.axis_size("ga")
    piece = pair_density.shape[1]
    rows = piece * NV
    first = (lax.axis_index("ka") * bands + lax.axis_index("band")) * piece
    local = perm_lists.reshape(-1, BLOCKS, GB) - (jnp.arange(BLOCKS, dtype=jnp.int32) * GB)[None, :, None]
    hit = local[:, :, :, None] == jnp.arange(GB, dtype=jnp.int32)
    inverse = jnp.sum(jnp.where(hit, jnp.arange(GB, dtype=jnp.int32)[:, None], 0), axis=2)
    inv_k = jnp.take(inverse.reshape(-1, NG), op_of_k, axis=0)
    cond_own = lax.dynamic_slice_in_dim(conduction_energy, first, piece, 1)
    diff = jnp.take(valence_energy, star_map, axis=0)[:, None, :] - jnp.take(cond_own, star_map, axis=0)[:, :, None]
    mask = ((first + jnp.arange(piece))[None, :] < cond_top[:, None]).astype(jnp.float32)[:, :, None]
    weight = 4.0 / KF * diff / (diff * diff) * mask
    w_row = weight.reshape(1, KF * rows)

    ct, chunk = 256, min(2048, KF * rows)
    mine = NG // gas
    partial_chi = pl.pallas_call(
        functools.partial(partial_kernel, rows, ct, chunk, bands, gas),
        grid_spec=pltpu.PrefetchScalarGridSpec(
            num_scalar_prefetch=1,
            grid=(NG // ct,),
            in_specs=[pl.BlockSpec(memory_space=pltpu.VMEM)] * 3,
            out_specs=pl.BlockSpec((mine, ct), lambda j, s: (0, j)),
            scratch_shapes=[pltpu.VMEM((NG, KF * rows), jnp.bfloat16)],
        ),
        out_shape=jax.ShapeDtypeStruct((mine, NG), jnp.float32),
        compiler_params=pltpu.CompilerParams(vmem_limit_bytes=56 * 1024 * 1024),
    )(star_map, pair_density.reshape(KI, rows, NG), inv_k, w_row)
    column_sums = lax.psum_scatter(partial_chi, "ka", scatter_dimension=1, tiled=True)
    return lax.psum_scatter(column_sums, "band", scatter_dimension=0, tiled=True)[None]


def solution(mesh):
    return jax.shard_map(
        on_device,
        mesh=mesh,
        in_specs=(P(None, ("ka", "band"), None, None), P(), P(), P(), P(), P(), P()),
        out_specs=P(None, ("band", "ga"), "ka"),
        check_vma=False,
    )
```

```python
import functools
import itertools

import jax
import jax.numpy as jnp
from jax import lax
from jax.experimental import pallas as pl
from jax.experimental.pallas import tpu as pltpu
from jax.sharding import PartitionSpec as P

NV = 8
NG = 2048
GB = 128
KI = 8
KF = 64
BLOCKS = NG // GB
NT = (((1,), (1,)), ((), ()))


def rotate_all(rows, star_ref, pd_ref, inv_ref, rot_ref):
    group = max(1, GB // rows)
    wide = group * rows
    targets = lax.broadcasted_iota(jnp.int32, (GB, GB), 0)

    def one_eight(e, carry):
        for sub, b in itertools.product(range(8 // group), range(BLOCKS)):
            start = pl.multiple_of(e * (8 * rows) + sub * wide, wide)
            cols = slice(b * GB, (b + 1) * GB)
            moved = None
            source = inv_ref[pl.ds(pl.multiple_of(e * 8, 8), 8), cols]
            pieces = [pd_ref[star_ref[e * 8 + sub * group + m], :, cols] for m in range(group)]
            for m in range(group):
                at = sub * group + m
                if group == 1:
                    x = pieces[0]
                else:
                    x = jnp.concatenate(
                        [p if n == m else jnp.zeros_like(p) for n, p in enumerate(pieces)], axis=0
                    )
                onehot = jnp.where(
                    source[at : at + 1] == targets, 1.0, 0.0
                ).astype(jnp.bfloat16)
                part = lax.dot_general(onehot, x, NT, preferred_element_type=jnp.float32)
                moved = part if moved is None else moved + part
            rot_ref[cols, pl.ds(start, wide)] = moved.astype(jnp.bfloat16)
        return carry

    lax.fori_loop(0, KF // 8, one_eight, 0)


def partial_kernel(rows, ct, chunk, bands, gas, star_ref, pd_ref, inv_ref, w_ref, out_ref, rot_ref):
    tile = pl.program_id(0)

    @pl.when(tile == 0)
    def rotate():
        rotate_all(rows, star_ref, pd_ref, inv_ref, rot_ref)

    slab = NG // (bands * gas)
    ga = lax.axis_index("ga")
    base = pl.multiple_of(tile * ct, ct)
    out_ref[...] = jnp.zeros_like(out_ref)

    def one_chunk(q, carry):
        ks = pl.ds(pl.multiple_of(q * chunk, chunk), chunk)
        scaled = (rot_ref[pl.ds(base, ct), ks].astype(jnp.float32) * w_ref[:, ks]).astype(jnp.bfloat16)
        for band in range(bands):
            left = rot_ref[pl.ds(pl.multiple_of((band * gas + ga) * slab, slab), slab), ks]
            out_ref[band * slab : (band + 1) * slab, :] += lax.dot_general(
                left, scaled, NT, preferred_element_type=jnp.float32
            )
        return carry

    lax.fori_loop(0, (KF * rows) // chunk, one_chunk, 0)


def send(source, target, out_sem, in_sem, device):
    return pltpu.make_async_remote_copy(
        src_ref=source,
        dst_ref=target,
        send_sem=out_sem,
        recv_sem=in_sem,
        device_id=device,
        device_id_type=pl.DeviceIdType.MESH,
    )


STEPS_Z = (2, 3, 1, 0)


def fused_kernel(
    rows, chunk, star_ref, pd_ref, inv_ref, w_ref, out_ref,
    rot_ref, acc, x_out, x_in, y_out, y_in, z_in,
    xs_sem, xr_sem, ys_sem, yr_sem, zs_sem, zr_sem,
):
    ka = lax.axis_index("ka")
    x = lax.axis_index("band")
    ga = lax.axis_index("ga")
    z, y = ka // 2, ka % 2
    to_x = {"band": 1 - x}
    to_y = {"ka": z * 2 + (1 - y)}
    to_z = [{"ka": ((z + step) % 4) * 2 + y} for step in STEPS_Z[:3]]
    barrier = pltpu.get_barrier_semaphore()
    for device in [to_x, to_y] + to_z:
        pl.semaphore_signal(barrier, inc=1, device_id=device, device_id_type=pl.DeviceIdType.MESH)
    pl.semaphore_wait(barrier, 5)

    rotate_all(rows, star_ref, pd_ref, inv_ref, rot_ref)

    slab, ct = out_ref.shape
    own_rows = pl.ds(pl.multiple_of((x * 2 + ga) * slab, slab), slab)
    far_rows = pl.ds(pl.multiple_of(((1 - x) * 2 + ga) * slab, slab), slab)

    def compute(t, z_to, y_to):
        base = pl.multiple_of((z_to * 2 + y_to) * ct, ct)
        acc[t] = jnp.zeros((slab, ct), jnp.float32)
        out_ref[...] = jnp.zeros((slab, ct), jnp.float32)

        def one_chunk(q, carry):
            ks = pl.ds(pl.multiple_of(q * chunk, chunk), chunk)
            scaled = (rot_ref[pl.ds(base, ct), ks].astype(jnp.float32) * w_ref[:, ks]).astype(jnp.bfloat16)
            out_ref[...] += lax.dot_general(rot_ref[far_rows, ks], scaled, NT, preferred_element_type=jnp.float32)
            acc[t] += lax.dot_general(rot_ref[own_rows, ks], scaled, NT, preferred_element_type=jnp.float32)
            return carry

        lax.fori_loop(0, (KF * rows) // chunk, one_chunk, 0)
        x_out[t] = out_ref[...].astype(jnp.bfloat16)

    x_copies = [send(x_out.at[t], x_in.at[t], xs_sem.at[t], xr_sem.at[t], to_x) for t in range(8)]
    y_copies = [send(y_out.at[i], y_in.at[i], ys_sem.at[i], yr_sem.at[i], to_y) for i in range(4)]
    z_copies = [send(acc.at[2 * i + 1], z_in.at[i], zs_sem.at[i], zr_sem.at[i], to_z[i]) for i in range(3)]

    def take_x(t):
        x_copies[t].wait_recv()
        acc[t] += x_in[t].astype(jnp.float32)
        if t % 2 == 0:
            y_out[t // 2] = acc[t].astype(jnp.bfloat16)
            y_copies[t // 2].start()

    def take_y(i):
        y_copies[i].wait_recv()
        acc[2 * i + 1] += y_in[i].astype(jnp.float32)
        if i < 3:
            z_copies[i].start()

    for t in range(8):
        i = t // 2
        compute(t, (z + STEPS_Z[i]) % 4, (1 - y) if t % 2 == 0 else y)
        x_copies[t].start()
        if t >= 1:
            take_x(t - 1)
            if t >= 3 and t % 2 == 1:
                take_y(i - 1)
    take_x(7)
    take_y(3)
    total = acc[7]
    for i in range(3):
        z_copies[i].wait_recv()
        total += z_in[i]
    out_ref[...] = total
    for copy in x_copies + y_copies + z_copies:
        copy.wait_send()


def fused(rows, star_map, pd, inv_k, w_row):
    slab, ct = 512, 256
    f32, bf16 = jnp.float32, jnp.bfloat16
    dma = pltpu.SemaphoreType.DMA
    return pl.pallas_call(
        functools.partial(fused_kernel, rows, 2048),
        in_specs=[pl.BlockSpec(memory_space=pltpu.SMEM)] + [pl.BlockSpec(memory_space=pltpu.VMEM)] * 3,
        out_specs=pl.BlockSpec(memory_space=pltpu.VMEM),
        out_shape=jax.ShapeDtypeStruct((slab, ct), f32),
        scratch_shapes=[
            pltpu.VMEM((NG, KF * rows), bf16),
            pltpu.VMEM((8, slab, ct), f32),
            pltpu.VMEM((8, slab, ct), bf16),
            pltpu.VMEM((8, slab, ct), bf16),
            pltpu.VMEM((4, slab, ct), bf16),
            pltpu.VMEM((4, slab, ct), bf16),
            pltpu.VMEM((3, slab, ct), f32),
            dma((8,)), dma((8,)), dma((4,)), dma((4,)), dma((3,)), dma((3,)),
        ],
        compiler_params=pltpu.CompilerParams(
            collective_id=0, has_side_effects=True, vmem_limit_bytes=60 * 1024 * 1024
        ),
    )(star_map, pd, inv_k, w_row)


def on_device(
    pair_density, valence_energy, conduction_energy, star_map, op_of_k, perm_lists, cond_top
):
    bands = lax.axis_size("band")
    gas = lax.axis_size("ga")
    piece = pair_density.shape[1]
    rows = piece * NV
    first = (lax.axis_index("ka") * bands + lax.axis_index("band")) * piece
    local = perm_lists.reshape(-1, BLOCKS, GB) - (jnp.arange(BLOCKS, dtype=jnp.int32) * GB)[None, :, None]
    hit = local[:, :, :, None] == jnp.arange(GB, dtype=jnp.int32)
    inverse = jnp.sum(jnp.where(hit, jnp.arange(GB, dtype=jnp.int32)[:, None], 0), axis=2)
    inv_k = jnp.take(inverse.reshape(-1, NG), op_of_k, axis=0)
    cond_own = lax.dynamic_slice_in_dim(conduction_energy, first, piece, 1)
    diff = jnp.take(valence_energy, star_map, axis=0)[:, None, :] - jnp.take(cond_own, star_map, axis=0)[:, :, None]
    mask = ((first + jnp.arange(piece))[None, :] < cond_top[:, None]).astype(jnp.float32)[:, :, None]
    weight = 4.0 / KF * diff / (diff * diff) * mask
    w_row = weight.reshape(1, KF * rows)

    if (lax.axis_size("ka"), bands, gas) == (8, 2, 2):
        return fused(rows, star_map, pair_density.reshape(KI, rows, NG), inv_k, w_row)[None]
    ct, chunk = 256, min(2048, KF * rows)
    mine = NG // gas
    partial_chi = pl.pallas_call(
        functools.partial(partial_kernel, rows, ct, chunk, bands, gas),
        grid_spec=pltpu.PrefetchScalarGridSpec(
            num_scalar_prefetch=1,
            grid=(NG // ct,),
            in_specs=[pl.BlockSpec(memory_space=pltpu.VMEM)] * 3,
            out_specs=pl.BlockSpec((mine, ct), lambda j, s: (0, j)),
            scratch_shapes=[pltpu.VMEM((NG, KF * rows), jnp.bfloat16)],
        ),
        out_shape=jax.ShapeDtypeStruct((mine, NG), jnp.float32),
        compiler_params=pltpu.CompilerParams(vmem_limit_bytes=56 * 1024 * 1024),
    )(star_map, pair_density.reshape(KI, rows, NG), inv_k, w_row)
    column_sums = lax.psum_scatter(partial_chi, "ka", scatter_dimension=1, tiled=True)
    return lax.psum_scatter(column_sums, "band", scatter_dimension=0, tiled=True)[None]


def solution(mesh):
    return jax.shard_map(
        on_device,
        mesh=mesh,
        in_specs=(P(None, ("ka", "band"), None, None), P(), P(), P(), P(), P(), P()),
        out_specs=P(None, ("band", "ga"), "ka"),
        check_vma=False,
    )
```

```python
import functools

import jax
import jax.numpy as jnp
from jax import lax
from jax.experimental import pallas as pl
from jax.experimental.pallas import tpu as pltpu
from jax.sharding import PartitionSpec as P

NV = 8
NG = 2048
GB = 128
KI = 8
KF = 64
BLOCKS = NG // GB
NT = (((1,), (1,)), ((), ()))


PAIR = GB // KF


def rotate_tile(rows, tile, star_ref, pd_ref, perm_ref, rot_ref):
    group = max(1, GB // rows)
    wide = group * rows
    slots = lax.broadcasted_iota(jnp.int32, (GB, GB), 1)
    source = perm_ref[:, pl.ds(pl.multiple_of(tile * GB, GB), GB)]
    for half in range(PAIR):
        cols = pl.ds(pl.multiple_of((tile * PAIR + half) * GB, GB), GB)
        for q in range(KF // group):
            moved = None
            pieces = [pd_ref[star_ref[q * group + m], :, cols] for m in range(group)]
            for m in range(group):
                lane = half * KF + q * group + m
                if group == 1:
                    x = pieces[0]
                else:
                    x = jnp.concatenate(
                        [p if n == m else jnp.zeros_like(p) for n, p in enumerate(pieces)], axis=0
                    )
                onehot = jnp.where(source[:, lane : lane + 1] == slots, 1.0, 0.0).astype(jnp.bfloat16)
                part = lax.dot_general(onehot, x, NT, preferred_element_type=jnp.float32)
                moved = part if moved is None else moved + part
            rot_ref[cols, q * wide : (q + 1) * wide] = moved.astype(jnp.bfloat16)


def partial_kernel(rows, ct, chunk, bands, gas, star_ref, pd_ref, perm_ref, w_ref, out_ref, rot_ref):
    tile = pl.program_id(0)

    @pl.when(tile == 0)
    def rotate():
        def one(i, carry):
            rotate_tile(rows, i, star_ref, pd_ref, perm_ref, rot_ref)
            return carry

        lax.fori_loop(0, BLOCKS // PAIR, one, 0)

    slab = NG // (bands * gas)
    ga = lax.axis_index("ga")
    base = pl.multiple_of(tile * ct, ct)
    out_ref[...] = jnp.zeros_like(out_ref)

    def one_chunk(q, carry):
        ks = pl.ds(pl.multiple_of(q * chunk, chunk), chunk)
        scaled = (rot_ref[pl.ds(base, ct), ks].astype(jnp.float32) * w_ref[:, ks]).astype(jnp.bfloat16)
        for band in range(bands):
            left = rot_ref[pl.ds(pl.multiple_of((band * gas + ga) * slab, slab), slab), ks]
            out_ref[band * slab : (band + 1) * slab, :] += lax.dot_general(
                left, scaled, NT, preferred_element_type=jnp.float32
            )
        return carry

    lax.fori_loop(0, (KF * rows) // chunk, one_chunk, 0)


def send(source, target, out_sem, in_sem, device):
    return pltpu.make_async_remote_copy(
        src_ref=source,
        dst_ref=target,
        send_sem=out_sem,
        recv_sem=in_sem,
        device_id=device,
        device_id_type=pl.DeviceIdType.MESH,
    )


STEPS_Z = (2, 3, 1, 0)
ORDER = (0, 1, 2, 4, 3, 6, 5, 7)


def fused_kernel(
    rows, chunk, star_ref, pd_ref, perm_ref, w_ref, out_ref,
    rot_ref, acc, x_out, x_in, y_in, z_in,
    xs_sem, xr_sem, ys_sem, yr_sem, zs_sem, zr_sem,
):
    ka = lax.axis_index("ka")
    x = lax.axis_index("band")
    ga = lax.axis_index("ga")
    z, y = ka // 2, ka % 2
    to_x = {"band": 1 - x}
    to_y = {"ka": z * 2 + (1 - y)}
    to_z = [{"ka": ((z + step) % 4) * 2 + y} for step in STEPS_Z[:3]]
    barrier = pltpu.get_barrier_semaphore()
    for device in [to_x, to_y] + to_z:
        pl.semaphore_signal(barrier, inc=1, device_id=device, device_id_type=pl.DeviceIdType.MESH)
    pl.semaphore_wait(barrier, 5)

    def rotate_pair(z_of):
        def one(i, carry):
            rotate_tile(rows, z_of * 2 + i, star_ref, pd_ref, perm_ref, rot_ref)
            return carry

        lax.fori_loop(0, 2, one, 0)

    def row_tile(i, carry):
        rotate_tile(rows, (i // 2) * 4 + ga * 2 + i % 2, star_ref, pd_ref, perm_ref, rot_ref)
        return carry

    lax.fori_loop(0, 4, row_tile, 0)

    slab, ct = out_ref.shape
    own_rows = pl.ds(pl.multiple_of((x * 2 + ga) * slab, slab), slab)
    far_rows = pl.ds(pl.multiple_of(((1 - x) * 2 + ga) * slab, slab), slab)

    def compute(t, z_to, y_to):
        base = pl.multiple_of((z_to * 2 + y_to) * ct, ct)
        acc[t] = jnp.zeros((slab, ct), jnp.float32)
        out_ref[...] = jnp.zeros((slab, ct), jnp.float32)

        def one_chunk(q, carry):
            ks = pl.ds(pl.multiple_of(q * chunk, chunk), chunk)
            scaled = (rot_ref[pl.ds(base, ct), ks].astype(jnp.float32) * w_ref[:, ks]).astype(jnp.bfloat16)
            out_ref[...] += lax.dot_general(rot_ref[far_rows, ks], scaled, NT, preferred_element_type=jnp.float32)
            acc[t] += lax.dot_general(rot_ref[own_rows, ks], scaled, NT, preferred_element_type=jnp.float32)
            return carry

        lax.fori_loop(0, (KF * rows) // chunk, one_chunk, 0)
        x_out[t] = out_ref[...].astype(jnp.bfloat16)

    x_copies = [send(x_out.at[t], x_in.at[t], xs_sem.at[t], xr_sem.at[t], to_x) for t in range(8)]
    y_copies = [send(acc.at[2 * i], y_in.at[i], ys_sem.at[i], yr_sem.at[i], to_y) for i in range(4)]
    z_copies = [send(acc.at[2 * i + 1], z_in.at[i], zs_sem.at[i], zr_sem.at[i], to_z[i]) for i in range(3)]

    def take_x(t):
        x_copies[t].wait_recv()
        acc[t] += x_in[t].astype(jnp.float32)
        if t % 2 == 0:
            y_copies[t // 2].start()

    def take_y(i):
        y_copies[i].wait_recv()
        acc[2 * i + 1] += y_in[i]
        if i < 3:
            z_copies[i].start()

    before, rotated, summed = None, set(), []
    for t in ORDER:
        i = t // 2
        z_of = (z + STEPS_Z[i]) % 4
        if i not in rotated:
            rotated.add(i)
            pl.when(z_of % 2 != ga)(functools.partial(rotate_pair, z_of))
        compute(t, z_of, (1 - y) if t % 2 == 0 else y)
        x_copies[t].start()
        if summed:
            take_y(summed.pop(0))
        if before is not None:
            take_x(before)
            if before % 2 == 1:
                summed.append(before // 2)
        before = t
    for i in summed:
        take_y(i)
    take_x(before)
    take_y(before // 2)
    total = acc[7]
    for i in range(3):
        z_copies[i].wait_recv()
        total += z_in[i]
    out_ref[...] = total
    for copy in x_copies + y_copies + z_copies:
        copy.wait_send()


def fused(rows, star_map, pd, perm_k, w_row):
    slab, ct = 512, 256
    f32, bf16 = jnp.float32, jnp.bfloat16
    dma = pltpu.SemaphoreType.DMA
    return pl.pallas_call(
        functools.partial(fused_kernel, rows, 2048),
        in_specs=[pl.BlockSpec(memory_space=pltpu.SMEM)] + [pl.BlockSpec(memory_space=pltpu.VMEM)] * 3,
        out_specs=pl.BlockSpec(memory_space=pltpu.VMEM),
        out_shape=jax.ShapeDtypeStruct((slab, ct), f32),
        scratch_shapes=[
            pltpu.VMEM((NG, KF * rows), bf16),
            pltpu.VMEM((8, slab, ct), f32),
            pltpu.VMEM((8, slab, ct), bf16),
            pltpu.VMEM((8, slab, ct), bf16),
            pltpu.VMEM((4, slab, ct), f32),
            pltpu.VMEM((3, slab, ct), f32),
            dma((8,)), dma((8,)), dma((4,)), dma((4,)), dma((3,)), dma((3,)),
        ],
        compiler_params=pltpu.CompilerParams(
            collective_id=0, has_side_effects=True, vmem_limit_bytes=60 * 1024 * 1024
        ),
    )(star_map, pd, perm_k, w_row)


def on_device(
    pair_density, valence_energy, conduction_energy, star_map, op_of_k, perm_lists, cond_top
):
    bands = lax.axis_size("band")
    gas = lax.axis_size("ga")
    piece = pair_density.shape[1]
    rows = piece * NV
    first = (lax.axis_index("ka") * bands + lax.axis_index("band")) * piece
    local = jnp.take(perm_lists.reshape(-1, BLOCKS, GB), op_of_k, axis=0)
    local = local - (jnp.arange(BLOCKS, dtype=jnp.int32) * GB)[None, :, None]
    perm_k = local.transpose(2, 1, 0).reshape(GB, BLOCKS * KF)
    cond_own = lax.dynamic_slice_in_dim(conduction_energy, first, piece, 1)
    diff = jnp.take(valence_energy, star_map, axis=0)[:, None, :] - jnp.take(cond_own, star_map, axis=0)[:, :, None]
    mask = ((first + jnp.arange(piece))[None, :] < cond_top[:, None]).astype(jnp.float32)[:, :, None]
    weight = 4.0 / KF * diff / (diff * diff) * mask
    w_row = weight.reshape(1, KF * rows)

    if (lax.axis_size("ka"), bands, gas) == (8, 2, 2):
        return fused(rows, star_map, pair_density.reshape(KI, rows, NG), perm_k, w_row)[None]
    ct, chunk = 256, min(2048, KF * rows)
    mine = NG // gas
    partial_chi = pl.pallas_call(
        functools.partial(partial_kernel, rows, ct, chunk, bands, gas),
        grid_spec=pltpu.PrefetchScalarGridSpec(
            num_scalar_prefetch=1,
            grid=(NG // ct,),
            in_specs=[pl.BlockSpec(memory_space=pltpu.VMEM)] * 3,
            out_specs=pl.BlockSpec((mine, ct), lambda j, s: (0, j)),
            scratch_shapes=[pltpu.VMEM((NG, KF * rows), jnp.bfloat16)],
        ),
        out_shape=jax.ShapeDtypeStruct((mine, NG), jnp.float32),
        compiler_params=pltpu.CompilerParams(vmem_limit_bytes=56 * 1024 * 1024),
    )(star_map, pair_density.reshape(KI, rows, NG), perm_k, w_row)
    column_sums = lax.psum_scatter(partial_chi, "ka", scatter_dimension=1, tiled=True)
    return lax.psum_scatter(column_sums, "band", scatter_dimension=0, tiled=True)[None]


def solution(mesh):
    return jax.shard_map(
        on_device,
        mesh=mesh,
        in_specs=(P(None, ("ka", "band"), None, None), P(), P(), P(), P(), P(), P()),
        out_specs=P(None, ("band", "ga"), "ka"),
        check_vma=False,
    )
```

```python
import functools

import jax
import jax.numpy as jnp
from jax import lax
from jax.experimental import pallas as pl
from jax.experimental.pallas import tpu as pltpu
from jax.sharding import PartitionSpec as P

NV = 8
NG = 2048
GB = 128
KI = 8
KF = 64
BLOCKS = NG // GB
NT = (((1,), (1,)), ((), ()))


PAIR = GB // KF


def rotate_tile(rows, tile, star_ref, pd_ref, perm_ref, rot_ref):
    group = max(1, GB // rows)
    wide = group * rows
    slots = lax.broadcasted_iota(jnp.int32, (GB, GB), 1)
    source = perm_ref[:, pl.ds(pl.multiple_of(tile * GB, GB), GB)]
    for half in range(PAIR):
        cols = pl.ds(pl.multiple_of((tile * PAIR + half) * GB, GB), GB)
        for q in range(KF // group):
            moved = None
            pieces = [pd_ref[star_ref[q * group + m], :, cols] for m in range(group)]
            for m in range(group):
                lane = half * KF + q * group + m
                if group == 1:
                    x = pieces[0]
                else:
                    x = jnp.concatenate(
                        [p if n == m else jnp.zeros_like(p) for n, p in enumerate(pieces)], axis=0
                    )
                onehot = jnp.where(source[:, lane : lane + 1] == slots, 1.0, 0.0).astype(jnp.bfloat16)
                part = lax.dot_general(onehot, x, NT, preferred_element_type=jnp.float32)
                moved = part if moved is None else moved + part
            rot_ref[cols, q * wide : (q + 1) * wide] = moved.astype(jnp.bfloat16)


def partial_kernel(rows, ct, chunk, bands, gas, star_ref, pd_ref, perm_ref, w_ref, out_ref, rot_ref):
    tile = pl.program_id(0)

    @pl.when(tile == 0)
    def rotate():
        def one(i, carry):
            rotate_tile(rows, i, star_ref, pd_ref, perm_ref, rot_ref)
            return carry

        lax.fori_loop(0, BLOCKS // PAIR, one, 0)

    slab = NG // (bands * gas)
    ga = lax.axis_index("ga")
    base = pl.multiple_of(tile * ct, ct)
    out_ref[...] = jnp.zeros_like(out_ref)

    def one_chunk(q, carry):
        ks = pl.ds(pl.multiple_of(q * chunk, chunk), chunk)
        scaled = (rot_ref[pl.ds(base, ct), ks].astype(jnp.float32) * w_ref[:, ks]).astype(jnp.bfloat16)
        for band in range(bands):
            left = rot_ref[pl.ds(pl.multiple_of((band * gas + ga) * slab, slab), slab), ks]
            out_ref[band * slab : (band + 1) * slab, :] += lax.dot_general(
                left, scaled, NT, preferred_element_type=jnp.float32
            )
        return carry

    lax.fori_loop(0, (KF * rows) // chunk, one_chunk, 0)


def send(source, target, out_sem, in_sem, device):
    return pltpu.make_async_remote_copy(
        src_ref=source,
        dst_ref=target,
        send_sem=out_sem,
        recv_sem=in_sem,
        device_id=device,
        device_id_type=pl.DeviceIdType.MESH,
    )


STEPS_Z = (2, 3, 1, 0)
ORDER = (0, 1, 2, 4, 3, 6, 5, 7)


def fused_kernel(
    rows, chunk, star_ref, pd_ref, perm_ref, w_ref, out_ref,
    rot_ref, acc, x_out, x_in, y_in, z_in,
    xs_sem, xr_sem, ys_sem, yr_sem, zs_sem, zr_sem,
):
    ka = lax.axis_index("ka")
    x = lax.axis_index("band")
    ga = lax.axis_index("ga")
    z, y = ka // 2, ka % 2
    to_x = {"band": 1 - x}
    to_y = {"ka": z * 2 + (1 - y)}
    to_z = [{"ka": ((z + step) % 4) * 2 + y} for step in STEPS_Z[:3]]
    barrier = pltpu.get_barrier_semaphore()
    for device in [to_x, to_y] + to_z:
        pl.semaphore_signal(barrier, inc=1, device_id=device, device_id_type=pl.DeviceIdType.MESH)
    pl.semaphore_wait(barrier, 5)

    def rotate_pair(z_of):
        def one(i, carry):
            rotate_tile(rows, z_of * 2 + i, star_ref, pd_ref, perm_ref, rot_ref)
            return carry

        lax.fori_loop(0, 2, one, 0)

    def row_tile(i, carry):
        rotate_tile(rows, (i // 2) * 4 + ga * 2 + i % 2, star_ref, pd_ref, perm_ref, rot_ref)
        return carry

    lax.fori_loop(0, 4, row_tile, 0)

    slab, ct = out_ref.shape
    own_rows = pl.ds(pl.multiple_of((x * 2 + ga) * slab, slab), slab)
    far_rows = pl.ds(pl.multiple_of(((1 - x) * 2 + ga) * slab, slab), slab)

    def compute(t, z_to, y_to):
        base = pl.multiple_of((z_to * 2 + y_to) * ct, ct)
        acc[t] = jnp.zeros((slab, ct), jnp.float32)
        out_ref[...] = jnp.zeros((slab, ct), jnp.float32)

        def one_chunk(q, carry):
            ks = pl.ds(pl.multiple_of(q * chunk, chunk), chunk)
            scaled = (rot_ref[pl.ds(base, ct), ks].astype(jnp.float32) * w_ref[:, ks]).astype(jnp.bfloat16)
            out_ref[...] += lax.dot_general(rot_ref[far_rows, ks], scaled, NT, preferred_element_type=jnp.float32)
            acc[t] += lax.dot_general(rot_ref[own_rows, ks], scaled, NT, preferred_element_type=jnp.float32)
            return carry

        lax.fori_loop(0, (KF * rows) // chunk, one_chunk, 0)
        x_out[t] = out_ref[...].astype(jnp.bfloat16)

    x_copies = [send(x_out.at[t], x_in.at[t], xs_sem.at[t], xr_sem.at[t], to_x) for t in range(8)]
    y_copies = [send(acc.at[2 * i], y_in.at[i], ys_sem.at[i], yr_sem.at[i], to_y) for i in range(4)]
    z_copies = [send(acc.at[2 * i + 1], z_in.at[i], zs_sem.at[i], zr_sem.at[i], to_z[i]) for i in range(3)]

    def take_x(t):
        x_copies[t].wait_recv()
        acc[t] += x_in[t].astype(jnp.float32)
        if t % 2 == 0:
            y_copies[t // 2].start()

    def take_y(i):
        y_copies[i].wait_recv()
        acc[2 * i + 1] += y_in[i]
        if i < 3:
            z_copies[i].start()

    before, rotated, summed = None, set(), []
    for t in ORDER:
        i = t // 2
        z_of = (z + STEPS_Z[i]) % 4
        if i not in rotated:
            rotated.add(i)
            pl.when(z_of % 2 != ga)(functools.partial(rotate_pair, z_of))
        compute(t, z_of, (1 - y) if t % 2 == 0 else y)
        x_copies[t].start()
        if summed:
            take_y(summed.pop(0))
        if before is not None:
            take_x(before)
            if before % 2 == 1:
                summed.append(before // 2)
        before = t
    for i in summed:
        take_y(i)
    take_x(before)
    take_y(before // 2)
    total = acc[7]
    for i in range(3):
        z_copies[i].wait_recv()
        total += z_in[i]
    out_ref[...] = total
    for copy in x_copies + y_copies + z_copies:
        copy.wait_send()


def fused(rows, star_map, pd, perm_k, w_row):
    slab, ct = 512, 256
    f32, bf16 = jnp.float32, jnp.bfloat16
    dma = pltpu.SemaphoreType.DMA
    return pl.pallas_call(
        functools.partial(fused_kernel, rows, min(4096, KF * rows)),
        in_specs=[pl.BlockSpec(memory_space=pltpu.SMEM)] + [pl.BlockSpec(memory_space=pltpu.VMEM)] * 3,
        out_specs=pl.BlockSpec(memory_space=pltpu.VMEM),
        out_shape=jax.ShapeDtypeStruct((slab, ct), f32),
        scratch_shapes=[
            pltpu.VMEM((NG, KF * rows), bf16),
            pltpu.VMEM((8, slab, ct), f32),
            pltpu.VMEM((8, slab, ct), bf16),
            pltpu.VMEM((8, slab, ct), bf16),
            pltpu.VMEM((4, slab, ct), f32),
            pltpu.VMEM((3, slab, ct), f32),
            dma((8,)), dma((8,)), dma((4,)), dma((4,)), dma((3,)), dma((3,)),
        ],
        compiler_params=pltpu.CompilerParams(
            collective_id=0, has_side_effects=True, vmem_limit_bytes=60 * 1024 * 1024
        ),
    )(star_map, pd, perm_k, w_row)


def on_device(
    pair_density, valence_energy, conduction_energy, star_map, op_of_k, perm_lists, cond_top
):
    bands = lax.axis_size("band")
    gas = lax.axis_size("ga")
    piece = pair_density.shape[1]
    rows = piece * NV
    first = (lax.axis_index("ka") * bands + lax.axis_index("band")) * piece
    local = jnp.take(perm_lists.reshape(-1, BLOCKS, GB), op_of_k, axis=0)
    local = local - (jnp.arange(BLOCKS, dtype=jnp.int32) * GB)[None, :, None]
    perm_k = local.transpose(2, 1, 0).reshape(GB, BLOCKS * KF)
    cond_own = lax.dynamic_slice_in_dim(conduction_energy, first, piece, 1)
    diff = jnp.take(valence_energy, star_map, axis=0)[:, None, :] - jnp.take(cond_own, star_map, axis=0)[:, :, None]
    mask = ((first + jnp.arange(piece))[None, :] < cond_top[:, None]).astype(jnp.float32)[:, :, None]
    weight = 4.0 / KF * diff / (diff * diff) * mask
    w_row = weight.reshape(1, KF * rows)

    if (lax.axis_size("ka"), bands, gas) == (8, 2, 2):
        return fused(rows, star_map, pair_density.reshape(KI, rows, NG), perm_k, w_row)[None]
    ct, chunk = 256, min(2048, KF * rows)
    mine = NG // gas
    partial_chi = pl.pallas_call(
        functools.partial(partial_kernel, rows, ct, chunk, bands, gas),
        grid_spec=pltpu.PrefetchScalarGridSpec(
            num_scalar_prefetch=1,
            grid=(NG // ct,),
            in_specs=[pl.BlockSpec(memory_space=pltpu.VMEM)] * 3,
            out_specs=pl.BlockSpec((mine, ct), lambda j, s: (0, j)),
            scratch_shapes=[pltpu.VMEM((NG, KF * rows), jnp.bfloat16)],
        ),
        out_shape=jax.ShapeDtypeStruct((mine, NG), jnp.float32),
        compiler_params=pltpu.CompilerParams(vmem_limit_bytes=56 * 1024 * 1024),
    )(star_map, pair_density.reshape(KI, rows, NG), perm_k, w_row)
    column_sums = lax.psum_scatter(partial_chi, "ka", scatter_dimension=1, tiled=True)
    return lax.psum_scatter(column_sums, "band", scatter_dimension=0, tiled=True)[None]


def solution(mesh):
    return jax.shard_map(
        on_device,
        mesh=mesh,
        in_specs=(P(None, ("ka", "band"), None, None), P(), P(), P(), P(), P(), P()),
        out_specs=P(None, ("band", "ga"), "ka"),
        check_vma=False,
    )
```
